32 devices in a mesh: orb: 8 (over y, x, core), grp: 4 (over z).
Axes of the slice: x: 2, y: 2, z: 4, core: 2. Of those that a mesh axis runs over, the one named last changes fastest.
Arguments:
- orbitals: bfloat16 [32, 64000], P(('orb', 'grp')), may hold values from -8 to 8
Outputs:
- projector: bfloat16 [32, 64000], P(('orb', 'grp'))
The draws below stay inside these ranges and needn't reach their ends.
All inputs are finite; a program needn't handle non-finite values.
Results may differ from the reference program's by a relative error of at most 0.0012.
The reference program's roundings to bfloat16 on the way (of `exchange` and `inverse`) count: a program that leaves them out, or rounds other values in their place, can miss the bound.
Values may be sent and summed in bfloat16 or wider, within the bound.
A program may use at most 64 MiB of HBM per device.

```python
import math
import jax
import jax.numpy as jnp
from jax import lax

GRID = 40
STEPS = 3
CELLS = 64000
N = 32
N_ORB = 8
N_GRP = 4


def draw_orbitals(key, part):
    noise_key = jax.random.fold_in(key, 11)
    scale_key = jax.random.fold_in(key, 23)
    field_key = jax.random.fold_in(key, 37)
    plane = (jnp.arange(CELLS, dtype=jnp.int32) // (GRID * GRID)).astype(jnp.float32)
    envelope = jnp.exp(0.5 * math.log(3.0) * plane / (GRID - 1))
    noise = jax.random.normal(noise_key, (N, CELLS), jnp.float32)
    shared = jax.random.normal(field_key, (1, CELLS), jnp.float32)
    mixed = 0.7 * shared + 0.7 * noise
    scales = jnp.exp(jax.random.uniform(scale_key, (N, 1), jnp.float32, math.log(0.7), math.log(1.4)))
    values = jnp.clip(mixed * scales * envelope[None, :], -8.0, 8.0)
    return values.astype(jnp.bfloat16)


def setup_inputs(seed: int = 0) -> dict:
    splits = jax.random.split(jax.random.key(seed), 2)
    orbitals = draw_orbitals(jax.random.fold_in(splits[1], 71), 0)
    return {"orbitals": orbitals}


def kernel_table(size):
    freq = jnp.arange(size, dtype=jnp.int32)
    signed = jnp.where(freq <= size // 2, freq, freq - size).astype(jnp.float32)
    wave = 2.0 * math.pi / size * signed
    square = wave * wave
    total = square[:, None, None] + square[None, :, None] + square[None, None, :]
    safe = jnp.where(total > 0, total, 1.0)
    return jnp.where(total > 0, 4.0 * (1.0 - jnp.exp(-0.25 * total)) / safe, 1.0)

def pair_terms(pair, kernel):
    target, source = pair
    density = target.astype(jnp.float32) * source.astype(jnp.float32)
    volume = density.reshape(-1, GRID, GRID, GRID)
    spectrum = jnp.fft.fftn(volume, axes=(1, 2, 3)) * kernel
    potential = jnp.real(jnp.fft.ifftn(spectrum, axes=(1, 2, 3))).astype(jnp.float32)
    return source.astype(jnp.float32) * potential.reshape(density.shape)

def factorize(margin):
    symmetric = 0.5 * (margin + margin.T)
    magnitude = jnp.abs(symmetric)
    gamma = jnp.mean(jnp.diagonal(magnitude)) + 1e-06
    regularized = jnp.diag(jnp.sum(magnitude, axis=1) + gamma) - symmetric
    factor = jnp.linalg.cholesky(regularized)
    identity = jnp.eye(symmetric.shape[0], dtype=jnp.float32)
    inverse = jax.scipy.linalg.solve_triangular(factor, identity, lower=True)
    return inverse.astype(jnp.bfloat16)

def reference(orbitals):
    kernel = kernel_table(GRID)
    blocks = orbitals.reshape(N_ORB, N_GRP, CELLS)
    exchange = jnp.zeros((N, CELLS), jnp.float32)
    for step in range(STEPS):
        sources = jnp.roll(blocks, step, axis=0)
        terms = lax.map(lambda pair: pair_terms(pair, kernel), (blocks, sources))
        exchange = exchange - terms.reshape(N, CELLS)
    compact = exchange.astype(jnp.bfloat16)
    margin = jnp.dot(orbitals.astype(jnp.float32), compact.T.astype(jnp.float32), preferred_element_type=jnp.float32) / CELLS
    inverse = factorize(margin)
    return jnp.dot(inverse.astype(jnp.float32), compact.astype(jnp.float32), preferred_element_type=jnp.float32).astype(jnp.bfloat16)
```

```python
import functools
import math

import jax
import jax.numpy as jnp
import ml_dtypes
import numpy as np
from jax import lax
from jax.experimental import pallas as pl
from jax.experimental.pallas import tpu as pltpu
from jax.sharding import PartitionSpec as P

STEPS = 3
LANES = 128
AXES = ("orb", "grp")


def shifted(value, axis, steps):
    count = lax.axis_size(axis)
    pairs = [(source, (source + steps) % count) for source in range(count)]
    return lax.ppermute(value, axis, pairs)


def halves(table):
    high = table.astype(ml_dtypes.bfloat16)
    low = (table - high.astype(np.float64)).astype(ml_dtypes.bfloat16)
    return high, low


@functools.lru_cache(maxsize=None)
def tables(size):
    index = np.arange(size)
    angle = 2.0 * math.pi / size * (index[:, None] * index[None, :] % size)
    table = np.cos(angle) + np.sin(angle)
    plane = halves(np.kron(table, table))
    line = np.zeros((LANES, LANES))
    block = np.kron(np.eye(STEPS), table)
    line[: block.shape[0], : block.shape[0]] = block
    line = np.concatenate(halves(line), axis=1)
    signed = np.where(index <= size // 2, index, index - size)
    square = (2.0 * math.pi / size * signed) ** 2
    total = square[:, None, None] + square[None, :, None] + square[None, None, :]
    safe = np.where(total > 0, total, 1.0)
    kernel = np.where(total > 0, 4.0 * (1.0 - np.exp(-0.25 * total)) / safe, 1.0) / size**3
    kernel = np.tile(kernel.reshape(size * size, size), (1, STEPS))
    spread = np.zeros((size * size, LANES), np.float32)
    spread[:, : kernel.shape[1]] = kernel
    return plane[0], plane[1], line, spread


def split(value):
    high = value.astype(jnp.bfloat16)
    return high, (value - high.astype(jnp.float32)).astype(jnp.bfloat16)


def dot(left, right):
    return jnp.dot(left, right, preferred_element_type=jnp.float32)


def line_transform(value, line):
    high, low = split(value)
    both = dot(high, line)
    return both[:, :LANES] + (both[:, LANES:] + dot(low, line[:, :LANES]))


def plane_transform(store, high_ref, low_ref, pair, rows, block, scale=None):
    for start in range(0, rows, block):
        here = pl.ds(start, block)
        both = dot(high_ref[here, :], pair[...])
        out = both[:, :LANES] + (both[:, LANES:] + dot(low_ref[here, :], pair[:, :LANES]))
        store[here, :] = out if scale is None else out * scale[here, :]


def put_pair(pair, value):
    high, low = split(value)
    pair[:, :LANES] = high
    pair[:, LANES:] = low


def exchange_body(size, *refs):
    parts = refs[:STEPS]
    high_ref, low_ref, line_ref, kernel_ref, out_ref, store, pair = refs[STEPS:]
    rows = size * size
    block = rows // 5 if rows % 40 == 0 else rows
    values = [part[...].astype(jnp.float32) for part in parts]
    spare = jnp.zeros((rows, LANES - STEPS * size), jnp.float32)
    source = jnp.concatenate(values + [spare], axis=1)
    target = jnp.concatenate([values[0]] * STEPS + [spare], axis=1)
    line = line_ref[...]
    put_pair(pair, line_transform(target * source, line))
    plane_transform(store, high_ref, low_ref, pair, rows, block, kernel_ref)
    put_pair(pair, store[...])
    plane_transform(store, high_ref, low_ref, pair, rows, block)
    term = source * line_transform(store[...], line)
    total = -term[:, :size]
    for step in range(1, STEPS):
        total = total - term[:, step * size : (step + 1) * size]
    out_ref[...] = total.astype(jnp.bfloat16)


def exchange_of(parts, size):
    rows = size * size
    high, low, line, kernel = tables(size)
    vmem = pl.BlockSpec(memory_space=pltpu.VMEM)
    return pl.pallas_call(
        functools.partial(exchange_body, size),
        out_shape=jax.ShapeDtypeStruct((rows, size), jnp.bfloat16),
        in_specs=[vmem] * (STEPS + 4),
        out_specs=vmem,
        scratch_shapes=[
            pltpu.VMEM((rows, LANES), jnp.float32),
            pltpu.VMEM((rows, 2 * LANES), jnp.bfloat16),
        ],
        compiler_params=pltpu.CompilerParams(vmem_limit_bytes=48 * 2**20),
    )(*parts, high, low, line, kernel)


def factorize(margin):
    symmetric = 0.5 * (margin + margin.T)
    magnitude = jnp.abs(symmetric)
    gamma = jnp.mean(jnp.diagonal(magnitude)) + 1e-06
    regularized = jnp.diag(jnp.sum(magnitude, axis=1) + gamma) - symmetric
    factor = jnp.linalg.cholesky(regularized)
    identity = jnp.eye(symmetric.shape[0], dtype=jnp.float32)
    inverse = jax.scipy.linalg.solve_triangular(factor, identity, lower=True)
    return inverse.astype(jnp.bfloat16)


def to_slabs(flat, count, width):
    padded = jnp.pad(flat, ((0, 0), (0, count * width - flat.shape[1])))
    return lax.all_to_all(
        padded.reshape(count, width), AXES, split_axis=0, concat_axis=0, tiled=True
    )


def shards(orbitals):
    cells = orbitals.shape[1]
    size = round(cells ** (1.0 / 3.0))
    count = lax.axis_size("orb") * lax.axis_size("grp")
    width = -(-cells // (count * LANES)) * LANES
    parts = [orbitals] + [shifted(orbitals, "orb", step) for step in range(1, STEPS)]
    parts = [part.reshape(size * size, size) for part in parts]
    compact = exchange_of(parts, size).reshape(1, cells)
    orbital_slab = to_slabs(orbitals, count, width)
    exchange_slab = to_slabs(compact, count, width)
    margin = lax.dot_general(
        orbital_slab, exchange_slab, (((1,), (1,)), ((), ())), preferred_element_type=jnp.float32
    )
    inverse = factorize(lax.psum(margin, AXES) / cells)
    projected = dot(inverse, exchange_slab).astype(jnp.bfloat16)
    back = lax.all_to_all(projected, AXES, split_axis=0, concat_axis=0, tiled=True)
    return back.reshape(1, count * width)[:, :cells]


def solution(mesh):
    spec = P(AXES, None)
    return jax.shard_map(shards, mesh=mesh, in_specs=(spec,), out_specs=spec, check_vma=False)
```

```python
import functools
import math

import jax
import jax.numpy as jnp
import ml_dtypes
import numpy as np
from jax import lax
from jax.experimental import pallas as pl
from jax.experimental.pallas import tpu as pltpu
from jax.sharding import PartitionSpec as P

STEPS = 3
LANES = 128
AXES = ("orb", "grp")


def shifted(value, axis, steps):
    count = lax.axis_size(axis)
    pairs = [(source, (source + steps) % count) for source in range(count)]
    return lax.ppermute(value, axis, pairs)


def halves(table):
    high = table.astype(ml_dtypes.bfloat16)
    low = (table - high.astype(np.float64)).astype(ml_dtypes.bfloat16)
    return high, low


@functools.lru_cache(maxsize=None)
def tables(size):
    index = np.arange(size)
    angle = 2.0 * math.pi / size * (index[:, None] * index[None, :] % size)
    table = np.cos(angle) + np.sin(angle)
    plane = halves(np.kron(table, table))
    line = np.zeros((LANES, LANES))
    block = np.kron(np.eye(STEPS), table)
    line[: block.shape[0], : block.shape[0]] = block
    line = np.concatenate(halves(line), axis=1)
    signed = np.where(index <= size // 2, index, index - size)
    square = (2.0 * math.pi / size * signed) ** 2
    total = square[:, None, None] + square[None, :, None] + square[None, None, :]
    safe = np.where(total > 0, total, 1.0)
    kernel = np.where(total > 0, 4.0 * (1.0 - np.exp(-0.25 * total)) / safe, 1.0) / size**3
    kernel = np.tile(kernel.reshape(size * size, size), (1, STEPS))
    spread = np.zeros((size * size, LANES), np.float32)
    spread[:, : kernel.shape[1]] = kernel
    return plane[0], plane[1], line, spread


def split(value):
    high = value.astype(jnp.bfloat16)
    return high, (value - high.astype(jnp.float32)).astype(jnp.bfloat16)


def dot(left, right):
    return jnp.dot(left, right, preferred_element_type=jnp.float32)


def line_transform(value, line):
    high, low = split(value)
    both = dot(high, line)
    return both[:, :LANES] + (both[:, LANES:] + dot(low, line[:, :LANES]))


def plane_transform(store, high_ref, low_ref, pair, rows, block, scale=None):
    for start in range(0, rows, block):
        here = pl.ds(start, block)
        both = dot(high_ref[here, :], pair[...])
        out = both[:, :LANES] + (both[:, LANES:] + dot(low_ref[here, :], pair[:, :LANES]))
        store[here, :] = out if scale is None else out * scale[here, :]


def put_pair(pair, value):
    high, low = split(value)
    pair[:, :LANES] = high
    pair[:, LANES:] = low


def exchange_body(size, *refs):
    parts = refs[:STEPS]
    high_ref, low_ref, line_ref, kernel_ref, out_ref, store, pair = refs[STEPS:]
    rows = size * size
    block = rows // 5 if rows % 40 == 0 else rows
    values = [part[...].astype(jnp.float32) for part in parts]
    spare = jnp.zeros((rows, LANES - STEPS * size), jnp.float32)
    source = jnp.concatenate(values + [spare], axis=1)
    target = jnp.concatenate([values[0]] * STEPS + [spare], axis=1)
    line = line_ref[...]
    put_pair(pair, line_transform(target * source, line))
    plane_transform(store, high_ref, low_ref, pair, rows, block, kernel_ref)
    put_pair(pair, store[...])
    plane_transform(store, high_ref, low_ref, pair, rows, block)
    term = source * line_transform(store[...], line)
    total = -term[:, :size]
    for step in range(1, STEPS):
        total = total - term[:, step * size : (step + 1) * size]
    out_ref[...] = total.astype(jnp.bfloat16)


def exchange_of(parts, size):
    rows = size * size
    high, low, line, kernel = tables(size)
    vmem = pl.BlockSpec(memory_space=pltpu.VMEM)
    return pl.pallas_call(
        functools.partial(exchange_body, size),
        out_shape=jax.ShapeDtypeStruct((rows, size), jnp.bfloat16),
        in_specs=[vmem] * (STEPS + 4),
        out_specs=vmem,
        scratch_shapes=[
            pltpu.VMEM((rows, LANES), jnp.float32),
            pltpu.VMEM((rows, 2 * LANES), jnp.bfloat16),
        ],
        compiler_params=pltpu.CompilerParams(vmem_limit_bytes=48 * 2**20),
    )(*parts, high, low, line, kernel)


def factorize(margin):
    symmetric = 0.5 * (margin + margin.T)
    magnitude = jnp.abs(symmetric)
    gamma = jnp.mean(jnp.diagonal(magnitude)) + 1e-06
    regularized = jnp.diag(jnp.sum(magnitude, axis=1) + gamma) - symmetric
    factor = jnp.linalg.cholesky(regularized)
    identity = jnp.eye(symmetric.shape[0], dtype=jnp.float32)
    inverse = jax.scipy.linalg.solve_triangular(factor, identity, lower=True)
    return inverse.astype(jnp.bfloat16)


def to_slabs(flat, count, width):
    padded = jnp.pad(flat, ((0, 0), (0, count * width - flat.shape[1])))
    return lax.all_to_all(
        padded.reshape(count, width), AXES, split_axis=0, concat_axis=0, tiled=True
    )


def invert(mat, work, n, cells):
    lanes = mat.shape[2]
    row = lax.broadcasted_iota(jnp.int32, (n, lanes), 0)
    column = lax.broadcasted_iota(jnp.int32, (n, lanes), 1)
    diagonal = row == column
    symmetric = mat[:, 0, :] * (0.5 / cells)
    magnitude = jnp.abs(symmetric)
    gamma = jnp.sum(jnp.where(diagonal, magnitude, 0.0)) / n + 1e-06
    total = jnp.sum(magnitude, axis=1, keepdims=True) + gamma
    work[:, :lanes] = jnp.where(diagonal, total, 0.0) - symmetric
    work[:, lanes:] = jnp.where(diagonal, 1.0, 0.0)
    wide_row = lax.broadcasted_iota(jnp.int32, (n, 1), 0)

    def eliminate(step, carry):
        pivot_row = work[pl.ds(step, 1), :]
        value = work[...]
        left = jnp.where(column == step, value[:, :lanes], 0.0)
        entries = jnp.sum(left, axis=1, keepdims=True)
        pivot = jnp.sum(
            jnp.where(column[:1] == step, pivot_row[:, :lanes], 0.0), axis=1, keepdims=True
        )
        ratio = jnp.where(wide_row > step, entries / pivot, 0.0)
        work[...] = value - ratio * pivot_row
        return carry

    lax.fori_loop(0, n, eliminate, 0)
    pivots = jnp.sum(jnp.where(diagonal, work[:, :lanes], 0.0), axis=1, keepdims=True)
    return (work[:, lanes:] * lax.rsqrt(pivots)).astype(jnp.bfloat16)


def flatten(wide, ref):
    wide[...] = ref[...].astype(jnp.float32)
    pieces = [wide[:, line, :] for line in range(wide.shape[1])]
    return jnp.concatenate(pieces, axis=1).astype(jnp.bfloat16)


def tail_body(count, groups, cells, orbital, exchange, back, orb_slab, exc_slab, wide, part, got,
              line, mat, work, proj, send_sem, recv_sem):
    n = count
    lanes = mat.shape[2]
    me = lax.axis_index("orb") * groups + lax.axis_index("grp")

    def device(step):
        other = lax.rem(me + step, count)
        return other, (lax.div(other, groups), lax.rem(other, groups))

    def each(action):
        def body(step, carry):
            action(*device(step))
            return carry

        lax.fori_loop(1, count, body, 0)

    def send(source, target, slot, other, place):
        pltpu.make_async_remote_copy(
            src_ref=source,
            dst_ref=target.at[me],
            send_sem=send_sem.at[slot],
            recv_sem=recv_sem.at[slot],
            device_id=place,
            device_id_type=pl.DeviceIdType.MESH,
        ).start()

    def wait(target, slot):
        most = target.at[pl.ds(0, count - 1)]
        pltpu.make_async_copy(most, most, recv_sem.at[slot]).wait()
        pltpu.make_async_copy(most, most, send_sem.at[slot]).wait()

    barrier = pltpu.get_barrier_semaphore()
    each(
        lambda other, place: pl.semaphore_signal(
            barrier, inc=1, device_id=place, device_id_type=pl.DeviceIdType.MESH
        )
    )
    pl.semaphore_wait(barrier, count - 1)

    def slabs(other, place):
        send(exchange.at[other], exc_slab, 0, other, place)
        send(orbital.at[other], orb_slab, 1, other, place)

    each(slabs)
    exc_slab[pl.ds(me, 1)] = exchange[pl.ds(me, 1)]
    orb_slab[pl.ds(me, 1)] = orbital[pl.ds(me, 1)]
    wait(exc_slab, 0)
    wait(orb_slab, 1)
    exc = flatten(wide, exc_slab)
    orb = flatten(wide, orb_slab)
    turned = (((1,), (1,)), ((), ()))
    both = lax.dot_general(orb, exc, turned, preferred_element_type=jnp.float32)
    both = both + lax.dot_general(exc, orb, turned, preferred_element_type=jnp.float32)
    if lanes > n:
        both = jnp.concatenate([both, jnp.zeros((n, lanes - n), jnp.float32)], axis=1)
    part[...] = jnp.broadcast_to(both[:, None, :], part.shape)
    each(lambda other, place: send(part.at[other], got, 2, other, place))
    got[pl.ds(me, 1)] = part[pl.ds(me, 1)]
    wait(got, 2)
    line[...] = jnp.sum(got[...], axis=0)
    each(lambda other, place: send(line, mat, 3, other, place))
    mat[pl.ds(me, 1)] = line[...][None]
    wait(mat, 3)
    inverse = invert(mat, work, n, cells)[:, :n]
    projected = dot(inverse, exc)
    for index in range(wide.shape[1]):
        wide[:, index, :] = projected[:, index * LANES : (index + 1) * LANES]
    proj[...] = wide[...].astype(jnp.bfloat16)
    each(lambda other, place: send(proj.at[other], back, 4, other, place))
    back[pl.ds(me, 1)] = proj[pl.ds(me, 1)]
    wait(back, 4)


def tail(orbital, exchange, cells):
    count, lines, _ = orbital.shape
    groups = lax.axis_size("grp")
    lanes = -(-count // LANES) * LANES
    vmem = pl.BlockSpec(memory_space=pltpu.VMEM)
    slab = pltpu.VMEM(orbital.shape, jnp.bfloat16)
    rows = pltpu.VMEM((count, 8, lanes), jnp.float32)
    return pl.pallas_call(
        functools.partial(tail_body, count, groups, cells),
        out_shape=jax.ShapeDtypeStruct(orbital.shape, jnp.bfloat16),
        in_specs=[vmem] * 2,
        out_specs=vmem,
        scratch_shapes=[
            slab,
            slab,
            pltpu.VMEM(orbital.shape, jnp.float32),
            rows,
            rows,
            pltpu.VMEM((8, lanes), jnp.float32),
            rows,
            pltpu.VMEM((count, 2 * lanes), jnp.float32),
            slab,
            pltpu.SemaphoreType.DMA((5,)),
            pltpu.SemaphoreType.DMA((5,)),
        ],
        compiler_params=pltpu.CompilerParams(
            collective_id=0, has_side_effects=True, vmem_limit_bytes=56 * 2**20
        ),
    )(orbital, exchange)


def to_pieces(flat, count, lines):
    tall = flat.reshape(-1, LANES)
    padded = jnp.pad(tall, ((0, count * lines - tall.shape[0]), (0, 0)))
    return padded.reshape(count, lines, LANES)


def shards(orbitals):
    cells = orbitals.shape[1]
    size = round(cells ** (1.0 / 3.0))
    count = lax.axis_size("orb") * lax.axis_size("grp")
    parts = [orbitals] + [shifted(orbitals, "orb", step) for step in range(1, STEPS)]
    parts = [part.reshape(size * size, size) for part in parts]
    compact = exchange_of(parts, size)
    if count <= LANES:
        lines = -(-cells // (count * LANES * 16)) * 16
        back = tail(to_pieces(orbitals, count, lines), to_pieces(compact, count, lines), cells)
        return back.reshape(count * lines, LANES)[: cells // LANES].reshape(1, cells)
    width = -(-cells // (count * LANES)) * LANES
    orbital_slab = to_slabs(orbitals, count, width)
    exchange_slab = to_slabs(compact.reshape(1, cells), count, width)
    margin = lax.dot_general(
        orbital_slab, exchange_slab, (((1,), (1,)), ((), ())), preferred_element_type=jnp.float32
    )
    inverse = factorize(lax.psum(margin, AXES) / cells)
    projected = dot(inverse, exchange_slab).astype(jnp.bfloat16)
    back = lax.all_to_all(projected, AXES, split_axis=0, concat_axis=0, tiled=True)
    return back.reshape(1, count * width)[:, :cells]


def solution(mesh):
    spec = P(AXES, None)
    return jax.shard_map(shards, mesh=mesh, in_specs=(spec,), out_specs=spec, check_vma=False)
```

```python
import functools
import math

import jax
import jax.numpy as jnp
import ml_dtypes
import numpy as np
from jax import lax
from jax.experimental import pallas as pl
from jax.experimental.pallas import tpu as pltpu
from jax.sharding import PartitionSpec as P

STEPS = 3
LANES = 128
AXES = ("orb", "grp")


def shifted(value, axis, steps):
    count = lax.axis_size(axis)
    pairs = [(source, (source + steps) % count) for source in range(count)]
    return lax.ppermute(value, axis, pairs)


def halves(table):
    high = table.astype(ml_dtypes.bfloat16)
    low = (table - high.astype(np.float64)).astype(ml_dtypes.bfloat16)
    return high, low


@functools.lru_cache(maxsize=None)
def tables(size):
    index = np.arange(size)
    angle = 2.0 * math.pi / size * (index[:, None] * index[None, :] % size)
    table = np.cos(angle) + np.sin(angle)
    plane = halves(np.kron(table, table))
    line = np.zeros((LANES, LANES))
    block = np.kron(np.eye(STEPS), table)
    line[: block.shape[0], : block.shape[0]] = block
    line = np.concatenate(halves(line), axis=1)
    signed = np.where(index <= size // 2, index, index - size)
    square = (2.0 * math.pi / size * signed) ** 2
    total = square[:, None, None] + square[None, :, None] + square[None, None, :]
    safe = np.where(total > 0, total, 1.0)
    kernel = np.where(total > 0, 4.0 * (1.0 - np.exp(-0.25 * total)) / safe, 1.0) / size**3
    kernel = np.tile(kernel.reshape(size * size, size), (1, STEPS))
    spread = np.zeros((size * size, LANES), np.float32)
    spread[:, : kernel.shape[1]] = kernel
    return plane[0], plane[1], line, spread


def split(value):
    high = value.astype(jnp.bfloat16)
    return high, (value - high.astype(jnp.float32)).astype(jnp.bfloat16)


def dot(left, right):
    return jnp.dot(left, right, preferred_element_type=jnp.float32)


def line_transform(value, line):
    high, low = split(value)
    both = dot(high, line)
    return both[:, :LANES] + (both[:, LANES:] + dot(low, line[:, :LANES]))


def plane_transform(store, high_ref, low_ref, pair, rows, block, scale=None):
    for start in range(0, rows, block):
        here = pl.ds(start, block)
        both = dot(high_ref[here, :], pair[...])
        out = both[:, :LANES] + (both[:, LANES:] + dot(low_ref[here, :], pair[:, :LANES]))
        store[here, :] = out if scale is None else out * scale[here, :]


def put_pair(pair, value):
    high, low = split(value)
    pair[:, :LANES] = high
    pair[:, LANES:] = low


def exchange_body(size, *refs):
    parts = refs[:STEPS]
    high_ref, low_ref, line_ref, kernel_ref, out_ref, store, pair = refs[STEPS:]
    rows = size * size
    block = rows // 5 if rows % 40 == 0 else rows
    values = [part[...].astype(jnp.float32) for part in parts]
    spare = jnp.zeros((rows, LANES - STEPS * size), jnp.float32)
    source = jnp.concatenate(values + [spare], axis=1)
    target = jnp.concatenate([values[0]] * STEPS + [spare], axis=1)
    line = line_ref[...]
    put_pair(pair, line_transform(target * source, line))
    plane_transform(store, high_ref, low_ref, pair, rows, block, kernel_ref)
    put_pair(pair, store[...])
    plane_transform(store, high_ref, low_ref, pair, rows, block)
    term = source * line_transform(store[...], line)
    total = -term[:, :size]
    for step in range(1, STEPS):
        total = total - term[:, step * size : (step + 1) * size]
    out_ref[...] = total.astype(jnp.bfloat16)


def exchange_of(parts, size):
    rows = size * size
    high, low, line, kernel = tables(size)
    vmem = pl.BlockSpec(memory_space=pltpu.VMEM)
    return pl.pallas_call(
        functools.partial(exchange_body, size),
        out_shape=jax.ShapeDtypeStruct((rows, size), jnp.bfloat16),
        in_specs=[vmem] * (STEPS + 4),
        out_specs=vmem,
        scratch_shapes=[
            pltpu.VMEM((rows, LANES), jnp.float32),
            pltpu.VMEM((rows, 2 * LANES), jnp.bfloat16),
        ],
        compiler_params=pltpu.CompilerParams(vmem_limit_bytes=48 * 2**20),
    )(*parts, high, low, line, kernel)


def factorize(margin):
    symmetric = 0.5 * (margin + margin.T)
    magnitude = jnp.abs(symmetric)
    gamma = jnp.mean(jnp.diagonal(magnitude)) + 1e-06
    regularized = jnp.diag(jnp.sum(magnitude, axis=1) + gamma) - symmetric
    factor = jnp.linalg.cholesky(regularized)
    identity = jnp.eye(symmetric.shape[0], dtype=jnp.float32)
    inverse = jax.scipy.linalg.solve_triangular(factor, identity, lower=True)
    return inverse.astype(jnp.bfloat16)


def to_slabs(flat, count, width):
    padded = jnp.pad(flat, ((0, 0), (0, count * width - flat.shape[1])))
    return lax.all_to_all(
        padded.reshape(count, width), AXES, split_axis=0, concat_axis=0, tiled=True
    )


def invert(symmetric, n):
    row = lax.broadcasted_iota(jnp.int32, (n, n), 0)
    column = lax.broadcasted_iota(jnp.int32, (n, n), 1)
    diagonal = row == column
    magnitude = jnp.abs(symmetric)
    gamma = jnp.sum(jnp.where(diagonal, magnitude, 0.0)) / n + 1e-06
    total = jnp.sum(magnitude, axis=1, keepdims=True) + gamma
    regularized = jnp.where(diagonal, total, 0.0) - symmetric
    value = jnp.concatenate([regularized, jnp.where(diagonal, 1.0, 0.0)], axis=1)
    below = lax.broadcasted_iota(jnp.int32, (n, 1), 0)
    for step in range(n - 1):
        here = slice(step, step + 1)
        scaled = value[here, :] / value[here, here]
        ratio = jnp.where(below > step, value[:, here], 0.0)
        value = value - ratio * scaled
    pivots = jnp.sum(jnp.where(diagonal, value[:, :n], 0.0), axis=1, keepdims=True)
    return (value[:, n:] * lax.rsqrt(pivots)).astype(jnp.bfloat16)


def flatten(wide, ref):
    wide[...] = ref[...].astype(jnp.float32)
    pieces = [wide[:, line, :] for line in range(wide.shape[1])]
    return jnp.concatenate(pieces, axis=1).astype(jnp.bfloat16)


def tail_body(count, groups, cells, orbital, exchange, back, orb_slab, exc_slab, wide, part, got,
              proj, send_sem, recv_sem):
    n = count
    me = lax.axis_index("orb") * groups + lax.axis_index("grp")

    def device(step):
        other = me + step
        other = jnp.where(other >= count, other - count, other)
        return other, (lax.div(other, groups), lax.rem(other, groups))

    def each(action):
        def body(step, carry):
            action(*device(step))
            return carry

        lax.fori_loop(1, count, body, 0)

    def send(source, target, slot, other, place):
        pltpu.make_async_remote_copy(
            src_ref=source,
            dst_ref=target.at[me],
            send_sem=send_sem.at[slot],
            recv_sem=recv_sem.at[slot],
            device_id=place,
            device_id_type=pl.DeviceIdType.MESH,
        ).start()

    def wait(target, slot):
        most = target.at[pl.ds(0, count - 1)]
        pltpu.make_async_copy(most, most, recv_sem.at[slot]).wait()
        pltpu.make_async_copy(most, most, send_sem.at[slot]).wait()

    barrier = pltpu.get_barrier_semaphore()
    each(
        lambda other, place: pl.semaphore_signal(
            barrier, inc=1, device_id=place, device_id_type=pl.DeviceIdType.MESH
        )
    )
    pl.semaphore_wait(barrier, count - 1)

    def slabs(other, place):
        send(exchange.at[other], exc_slab, 0, other, place)
        send(orbital.at[other], orb_slab, 1, other, place)

    each(slabs)
    exc_slab[pl.ds(me, 1)] = exchange[pl.ds(me, 1)]
    orb_slab[pl.ds(me, 1)] = orbital[pl.ds(me, 1)]
    wait(exc_slab, 0)
    wait(orb_slab, 1)
    exc = flatten(wide, exc_slab)
    orb = flatten(wide, orb_slab)
    turned = (((1,), (1,)), ((), ()))
    both = lax.dot_general(orb, exc, turned, preferred_element_type=jnp.float32)
    both = both + lax.dot_general(exc, orb, turned, preferred_element_type=jnp.float32)
    both = both * (0.5 / cells)
    part[...] = jnp.concatenate([both[top : top + 8, :] for top in range(0, n, 8)], axis=1)
    each(lambda other, place: send(part, got, 2, other, place))
    got[pl.ds(me, 1)] = part[...][None]
    wait(got, 2)
    summed = jnp.sum(got[...], axis=0)
    symmetric = jnp.concatenate([summed[:, left : left + n] for left in range(0, n * n // 8, n)], axis=0)
    inverse = invert(symmetric, n)
    projected = dot(inverse, exc)
    for index in range(wide.shape[1]):
        wide[:, index, :] = projected[:, index * LANES : (index + 1) * LANES]
    proj[...] = wide[...].astype(jnp.bfloat16)
    each(lambda other, place: send(proj.at[other], back, 3, other, place))
    back[pl.ds(me, 1)] = proj[pl.ds(me, 1)]
    wait(back, 3)


def tail(orbital, exchange, cells):
    count, lines, _ = orbital.shape
    groups = lax.axis_size("grp")
    packed = count * count // 8
    vmem = pl.BlockSpec(memory_space=pltpu.VMEM)
    slab = pltpu.VMEM(orbital.shape, jnp.bfloat16)
    return pl.pallas_call(
        functools.partial(tail_body, count, groups, cells),
        out_shape=jax.ShapeDtypeStruct(orbital.shape, jnp.bfloat16),
        in_specs=[vmem] * 2,
        out_specs=vmem,
        scratch_shapes=[
            slab,
            slab,
            pltpu.VMEM(orbital.shape, jnp.float32),
            pltpu.VMEM((8, packed), jnp.float32),
            pltpu.VMEM((count, 8, packed), jnp.float32),
            slab,
            pltpu.SemaphoreType.DMA((4,)),
            pltpu.SemaphoreType.DMA((4,)),
        ],
        compiler_params=pltpu.CompilerParams(
            collective_id=0, has_side_effects=True, vmem_limit_bytes=56 * 2**20
        ),
    )(orbital, exchange)


def to_pieces(flat, count, lines):
    tall = flat.reshape(-1, LANES)
    padded = jnp.pad(tall, ((0, count * lines - tall.shape[0]), (0, 0)))
    return padded.reshape(count, lines, LANES)


def shards(orbitals):
    cells = orbitals.shape[1]
    size = round(cells ** (1.0 / 3.0))
    count = lax.axis_size("orb") * lax.axis_size("grp")
    parts = [orbitals] + [shifted(orbitals, "orb", step) for step in range(1, STEPS)]
    parts = [part.reshape(size * size, size) for part in parts]
    compact = exchange_of(parts, size)
    if count <= LANES // 2 and count % 32 == 0:
        lines = -(-cells // (count * LANES * 16)) * 16
        back = tail(to_pieces(orbitals, count, lines), to_pieces(compact, count, lines), cells)
        return back.reshape(count * lines, LANES)[: cells // LANES].reshape(1, cells)
    width = -(-cells // (count * LANES)) * LANES
    orbital_slab = to_slabs(orbitals, count, width)
    exchange_slab = to_slabs(compact.reshape(1, cells), count, width)
    margin = lax.dot_general(
        orbital_slab, exchange_slab, (((1,), (1,)), ((), ())), preferred_element_type=jnp.float32
    )
    inverse = factorize(lax.psum(margin, AXES) / cells)
    projected = dot(inverse, exchange_slab).astype(jnp.bfloat16)
    back = lax.all_to_all(projected, AXES, split_axis=0, concat_axis=0, tiled=True)
    return back.reshape(1, count * width)[:, :cells]


def solution(mesh):
    spec = P(AXES, None)
    return jax.shard_map(shards, mesh=mesh, in_specs=(spec,), out_specs=spec, check_vma=False)
```

```python
import functools
import math

import jax
import jax.numpy as jnp
import ml_dtypes
import numpy as np
from jax import lax
from jax.experimental import pallas as pl
from jax.experimental.pallas import tpu as pltpu
from jax.sharding import PartitionSpec as P

STEPS = 3
LANES = 128
AXES = ("orb", "grp")


def shifted(value, axis, steps):
    count = lax.axis_size(axis)
    pairs = [(source, (source + steps) % count) for source in range(count)]
    return lax.ppermute(value, axis, pairs)


def halves(table):
    high = table.astype(ml_dtypes.bfloat16)
    low = (table - high.astype(np.float64)).astype(ml_dtypes.bfloat16)
    return high, low


@functools.lru_cache(maxsize=None)
def tables(size):
    index = np.arange(size)
    angle = 2.0 * math.pi / size * (index[:, None] * index[None, :] % size)
    table = np.cos(angle) + np.sin(angle)
    plane = halves(np.kron(table, table))
    line = np.zeros((LANES, LANES))
    block = np.kron(np.eye(STEPS), table)
    line[: block.shape[0], : block.shape[0]] = block
    line = np.concatenate(halves(line), axis=1)
    signed = np.where(index <= size // 2, index, index - size)
    square = (2.0 * math.pi / size * signed) ** 2
    total = square[:, None, None] + square[None, :, None] + square[None, None, :]
    safe = np.where(total > 0, total, 1.0)
    kernel = np.where(total > 0, 4.0 * (1.0 - np.exp(-0.25 * total)) / safe, 1.0) / size**3
    kernel = np.tile(kernel.reshape(size * size, size), (1, STEPS))
    spread = np.zeros((size * size, LANES), np.float32)
    spread[:, : kernel.shape[1]] = kernel
    return plane[0], plane[1], line, spread


def split(value):
    high = value.astype(jnp.bfloat16)
    return high, (value - high.astype(jnp.float32)).astype(jnp.bfloat16)


def dot(left, right):
    return jnp.dot(left, right, preferred_element_type=jnp.float32)


def line_transform(value, line):
    high, low = split(value)
    both = dot(high, line)
    return both[:, :LANES] + (both[:, LANES:] + dot(low, line[:, :LANES]))


def plane_transform(store, high_ref, low_ref, pair, rows, block, scale=None):
    for start in range(0, rows, block):
        here = pl.ds(start, block)
        both = dot(high_ref[here, :], pair[...])
        out = both[:, :LANES] + (both[:, LANES:] + dot(low_ref[here, :], pair[:, :LANES]))
        store[here, :] = out if scale is None else out * scale[here, :]


def put_pair(pair, value):
    high, low = split(value)
    pair[:, :LANES] = high
    pair[:, LANES:] = low


def exchange_body(size, *refs):
    parts = refs[:STEPS]
    high_ref, low_ref, line_ref, kernel_ref, out_ref, store, pair = refs[STEPS:]
    rows = size * size
    block = rows // 5 if rows % 40 == 0 else rows
    values = [part[...].astype(jnp.float32) for part in parts]
    spare = jnp.zeros((rows, LANES - STEPS * size), jnp.float32)
    source = jnp.concatenate(values + [spare], axis=1)
    target = jnp.concatenate([values[0]] * STEPS + [spare], axis=1)
    line = line_ref[...]
    put_pair(pair, line_transform(target * source, line))
    plane_transform(store, high_ref, low_ref, pair, rows, block, kernel_ref)
    put_pair(pair, store[...])
    plane_transform(store, high_ref, low_ref, pair, rows, block)
    term = source * line_transform(store[...], line)
    total = -term[:, :size]
    for step in range(1, STEPS):
        total = total - term[:, step * size : (step + 1) * size]
    out_ref[...] = total.astype(jnp.bfloat16)


def exchange_of(parts, size):
    rows = size * size
    high, low, line, kernel = tables(size)
    vmem = pl.BlockSpec(memory_space=pltpu.VMEM)
    return pl.pallas_call(
        functools.partial(exchange_body, size),
        out_shape=jax.ShapeDtypeStruct((rows, size), jnp.bfloat16),
        in_specs=[vmem] * (STEPS + 4),
        out_specs=vmem,
        scratch_shapes=[
            pltpu.VMEM((rows, LANES), jnp.float32),
            pltpu.VMEM((rows, 2 * LANES), jnp.bfloat16),
        ],
        compiler_params=pltpu.CompilerParams(vmem_limit_bytes=48 * 2**20),
    )(*parts, high, low, line, kernel)


class Peers:
    def __init__(self, count, groups, send_sem, recv_sem):
        self.count, self.groups = count, groups
        self.send_sem, self.recv_sem = send_sem, recv_sem
        self.me = lax.axis_index("orb") * groups + lax.axis_index("grp")

    def each(self, action):
        def body(step, carry):
            other = self.me + step
            other = jnp.where(other >= self.count, other - self.count, other)
            action(other, (lax.div(other, self.groups), lax.rem(other, self.groups)))
            return carry

        lax.fori_loop(1, self.count, body, 0, unroll=True)

    def greet(self):
        barrier = pltpu.get_barrier_semaphore()
        self.each(
            lambda other, place: pl.semaphore_signal(
                barrier, inc=1, device_id=place, device_id_type=pl.DeviceIdType.MESH
            )
        )
        pl.semaphore_wait(barrier, self.count - 1)

    def send(self, source, target, slot, place):
        pltpu.make_async_remote_copy(
            src_ref=source,
            dst_ref=target.at[self.me],
            send_sem=self.send_sem.at[slot],
            recv_sem=self.recv_sem.at[slot],
            device_id=place,
            device_id_type=pl.DeviceIdType.MESH,
        ).start()

    def wait(self, target, slot):
        most = target.at[pl.ds(0, self.count - 1)]
        pltpu.make_async_copy(most, most, self.recv_sem.at[slot]).wait()
        pltpu.make_async_copy(most, most, self.send_sem.at[slot]).wait()


def scatter_body(size, count, groups, *refs):
    pieces, local, (out_ref, slab_out), rest = refs[0], refs[1 : STEPS + 5], refs[STEPS + 5 : STEPS + 7], refs[STEPS + 7 :]
    store, pair, slab, send_sem, recv_sem = rest
    peers = Peers(count, groups, send_sem, recv_sem)
    peers.greet()
    peers.each(lambda other, place: peers.send(pieces.at[other], slab, 0, place))
    slab[pl.ds(peers.me, 1)] = pieces[pl.ds(peers.me, 1)]
    exchange_body(size, *local, out_ref, store, pair)
    peers.wait(slab, 0)
    slab_out[...] = slab[...]


def exchange_and_scatter(pieces, parts, size):
    rows = size * size
    high, low, line, kernel = tables(size)
    vmem = pl.BlockSpec(memory_space=pltpu.VMEM)
    return pl.pallas_call(
        functools.partial(scatter_body, size, pieces.shape[0], lax.axis_size("grp")),
        out_shape=(
            jax.ShapeDtypeStruct((rows, size), jnp.bfloat16),
            jax.ShapeDtypeStruct(pieces.shape, jnp.bfloat16),
        ),
        in_specs=[vmem] * (STEPS + 5),
        out_specs=(vmem, vmem),
        scratch_shapes=[
            pltpu.VMEM((rows, LANES), jnp.float32),
            pltpu.VMEM((rows, 2 * LANES), jnp.bfloat16),
            pltpu.VMEM(pieces.shape, jnp.bfloat16),
            pltpu.SemaphoreType.DMA((1,)),
            pltpu.SemaphoreType.DMA((1,)),
        ],
        compiler_params=pltpu.CompilerParams(
            collective_id=1, has_side_effects=True, vmem_limit_bytes=48 * 2**20
        ),
    )(pieces, *parts, high, low, line, kernel)


def factorize(margin):
    symmetric = 0.5 * (margin + margin.T)
    magnitude = jnp.abs(symmetric)
    gamma = jnp.mean(jnp.diagonal(magnitude)) + 1e-06
    regularized = jnp.diag(jnp.sum(magnitude, axis=1) + gamma) - symmetric
    factor = jnp.linalg.cholesky(regularized)
    identity = jnp.eye(symmetric.shape[0], dtype=jnp.float32)
    inverse = jax.scipy.linalg.solve_triangular(factor, identity, lower=True)
    return inverse.astype(jnp.bfloat16)


def to_slabs(flat, count, width):
    padded = jnp.pad(flat, ((0, 0), (0, count * width - flat.shape[1])))
    return lax.all_to_all(
        padded.reshape(count, width), AXES, split_axis=0, concat_axis=0, tiled=True
    )


def invert(symmetric, n):
    row = lax.broadcasted_iota(jnp.int32, (n, n), 0)
    column = lax.broadcasted_iota(jnp.int32, (n, n), 1)
    diagonal = row == column
    magnitude = jnp.abs(symmetric)
    gamma = jnp.sum(jnp.where(diagonal, magnitude, 0.0)) / n + 1e-06
    total = jnp.sum(magnitude, axis=1, keepdims=True) + gamma
    regularized = jnp.where(diagonal, total, 0.0) - symmetric
    value = jnp.concatenate([regularized, jnp.where(diagonal, 1.0, 0.0)], axis=1)
    below = lax.broadcasted_iota(jnp.int32, (n, 1), 0)
    for step in range(n - 1):
        here = slice(step, step + 1)
        scaled = value[here, :] / value[here, here]
        ratio = jnp.where(below > step, value[:, here], 0.0)
        value = value - ratio * scaled
    pivots = jnp.sum(jnp.where(diagonal, value[:, :n], 0.0), axis=1, keepdims=True)
    return (value[:, n:] * lax.rsqrt(pivots)).astype(jnp.bfloat16)


def flatten(wide, ref):
    wide[...] = ref[...].astype(jnp.float32)
    pieces = [wide[:, line, :] for line in range(wide.shape[1])]
    return jnp.concatenate(pieces, axis=1).astype(jnp.bfloat16)


def tail_body(count, groups, cells, orbital, exchange, back, exc_slab, wide, part, got, proj,
              send_sem, recv_sem):
    n = count
    peers = Peers(count, groups, send_sem, recv_sem)
    me = peers.me
    peers.greet()
    peers.each(lambda other, place: peers.send(exchange.at[other], exc_slab, 0, place))
    exc_slab[pl.ds(me, 1)] = exchange[pl.ds(me, 1)]
    orb = flatten(wide, orbital)
    peers.wait(exc_slab, 0)
    exc = flatten(wide, exc_slab)
    turned = (((1,), (1,)), ((), ()))
    both = lax.dot_general(orb, exc, turned, preferred_element_type=jnp.float32)
    both = both + lax.dot_general(exc, orb, turned, preferred_element_type=jnp.float32)
    both = both * (0.5 / cells)
    part[...] = jnp.concatenate([both[top : top + 8, :] for top in range(0, n, 8)], axis=1)
    peers.each(lambda other, place: peers.send(part, got, 1, place))
    got[pl.ds(me, 1)] = part[...][None]
    peers.wait(got, 1)
    summed = jnp.sum(got[...], axis=0)
    symmetric = jnp.concatenate([summed[:, left : left + n] for left in range(0, n * n // 8, n)], axis=0)
    inverse = invert(symmetric, n)
    projected = dot(inverse, exc)
    for index in range(wide.shape[1]):
        wide[:, index, :] = projected[:, index * LANES : (index + 1) * LANES]
    proj[...] = wide[...].astype(jnp.bfloat16)
    peers.each(lambda other, place: peers.send(proj.at[other], back, 2, place))
    back[pl.ds(me, 1)] = proj[pl.ds(me, 1)]
    peers.wait(back, 2)


def tail(orbital, exchange, cells):
    count, lines, _ = orbital.shape
    groups = lax.axis_size("grp")
    packed = count * count // 8
    vmem = pl.BlockSpec(memory_space=pltpu.VMEM)
    slab = pltpu.VMEM(orbital.shape, jnp.bfloat16)
    return pl.pallas_call(
        functools.partial(tail_body, count, groups, cells),
        out_shape=jax.ShapeDtypeStruct(orbital.shape, jnp.bfloat16),
        in_specs=[vmem] * 2,
        out_specs=vmem,
        scratch_shapes=[
            slab,
            pltpu.VMEM(orbital.shape, jnp.float32),
            pltpu.VMEM((8, packed), jnp.float32),
            pltpu.VMEM((count, 8, packed), jnp.float32),
            slab,
            pltpu.SemaphoreType.DMA((3,)),
            pltpu.SemaphoreType.DMA((3,)),
        ],
        compiler_params=pltpu.CompilerParams(
            collective_id=0, has_side_effects=True, vmem_limit_bytes=56 * 2**20
        ),
    )(orbital, exchange)


def to_pieces(flat, count, lines):
    tall = flat.reshape(-1, LANES)
    padded = jnp.pad(tall, ((0, count * lines - tall.shape[0]), (0, 0)))
    return padded.reshape(count, lines, LANES)


def shards(orbitals):
    cells = orbitals.shape[1]
    size = round(cells ** (1.0 / 3.0))
    count = lax.axis_size("orb") * lax.axis_size("grp")
    parts = [orbitals] + [shifted(orbitals, "orb", step) for step in range(1, STEPS)]
    parts = [part.reshape(size * size, size) for part in parts]
    if count <= LANES // 2 and count % 32 == 0:
        lines = -(-cells // (count * LANES * 16)) * 16
        compact, slab = exchange_and_scatter(to_pieces(orbitals, count, lines), parts, size)
        back = tail(slab, to_pieces(compact, count, lines), cells)
        return back.reshape(count * lines, LANES)[: cells // LANES].reshape(1, cells)
    compact = exchange_of(parts, size)
    width = -(-cells // (count * LANES)) * LANES
    orbital_slab = to_slabs(orbitals, count, width)
    exchange_slab = to_slabs(compact.reshape(1, cells), count, width)
    margin = lax.dot_general(
        orbital_slab, exchange_slab, (((1,), (1,)), ((), ())), preferred_element_type=jnp.float32
    )
    inverse = factorize(lax.psum(margin, AXES) / cells)
    projected = dot(inverse, exchange_slab).astype(jnp.bfloat16)
    back = lax.all_to_all(projected, AXES, split_axis=0, concat_axis=0, tiled=True)
    return back.reshape(1, count * width)[:, :cells]


def solution(mesh):
    spec = P(AXES, None)
    return jax.shard_map(shards, mesh=mesh, in_specs=(spec,), out_specs=spec, check_vma=False)
```

```python
import functools
import math

import jax
import jax.numpy as jnp
import ml_dtypes
import numpy as np
from jax import lax
from jax.experimental import pallas as pl
from jax.experimental.pallas import tpu as pltpu
from jax.sharding import PartitionSpec as P

STEPS = 3
LANES = 128
AXES = ("orb", "grp")


def shifted(value, axis, steps):
    count = lax.axis_size(axis)
    pairs = [(source, (source + steps) % count) for source in range(count)]
    return lax.ppermute(value, axis, pairs)


def halves(table):
    high = table.astype(ml_dtypes.bfloat16)
    low = (table - high.astype(np.float64)).astype(ml_dtypes.bfloat16)
    return high, low


@functools.lru_cache(maxsize=None)
def tables(size):
    index = np.arange(size)
    angle = 2.0 * math.pi / size * (index[:, None] * index[None, :] % size)
    table = np.cos(angle) + np.sin(angle)
    plane = halves(np.kron(table, table))
    line = np.zeros((LANES, LANES))
    block = np.kron(np.eye(STEPS), table)
    line[: block.shape[0], : block.shape[0]] = block
    line = np.concatenate(halves(line), axis=1)
    signed = np.where(index <= size // 2, index, index - size)
    square = (2.0 * math.pi / size * signed) ** 2
    total = square[:, None, None] + square[None, :, None] + square[None, None, :]
    safe = np.where(total > 0, total, 1.0)
    kernel = np.where(total > 0, 4.0 * (1.0 - np.exp(-0.25 * total)) / safe, 1.0) / size**3
    kernel = np.tile(kernel.reshape(size * size, size), (1, STEPS))
    spread = np.zeros((size * size, LANES), np.float32)
    spread[:, : kernel.shape[1]] = kernel
    return plane[0], plane[1], line, spread


def split(value):
    high = value.astype(jnp.bfloat16)
    return high, (value - high.astype(jnp.float32)).astype(jnp.bfloat16)


def dot(left, right):
    return jnp.dot(left, right, preferred_element_type=jnp.float32)


def line_transform(value, line):
    high, low = split(value)
    both = dot(high, line)
    return both[:, :LANES] + (both[:, LANES:] + dot(low, line[:, :LANES]))


def plane_transform(store, high_ref, low_ref, pair, rows, block, scale=None):
    for start in range(0, rows, block):
        here = pl.ds(start, block)
        both = dot(high_ref[here, :], pair[...])
        out = both[:, :LANES] + (both[:, LANES:] + dot(low_ref[here, :], pair[:, :LANES]))
        store[here, :] = out if scale is None else out * scale[here, :]


def put_pair(pair, value):
    high, low = split(value)
    pair[:, :LANES] = high
    pair[:, LANES:] = low


def exchange_body(size, *refs):
    parts = refs[:STEPS]
    high_far, low_far, line_ref, kernel_ref, out_ref, store, pair, high_ref, low_ref, sems = refs[STEPS:]
    copies = [
        pltpu.make_async_copy(high_far, high_ref, sems.at[0]),
        pltpu.make_async_copy(low_far, low_ref, sems.at[1]),
    ]
    for copy in copies:
        copy.start()
    rows = size * size
    block = rows // 5 if rows % 40 == 0 else rows
    values = [part[...].astype(jnp.float32) for part in parts]
    spare = jnp.zeros((rows, LANES - STEPS * size), jnp.float32)
    source = jnp.concatenate(values + [spare], axis=1)
    target = jnp.concatenate([values[0]] * STEPS + [spare], axis=1)
    line = line_ref[...]
    put_pair(pair, line_transform(target * source, line))
    for copy in copies:
        copy.wait()
    plane_transform(store, high_ref, low_ref, pair, rows, block, kernel_ref)
    put_pair(pair, store[...])
    plane_transform(store, high_ref, low_ref, pair, rows, block)
    term = source * line_transform(store[...], line)
    total = -term[:, :size]
    for step in range(1, STEPS):
        total = total - term[:, step * size : (step + 1) * size]
    out_ref[...] = total.astype(jnp.bfloat16)


def exchange_of(parts, size):
    rows = size * size
    high, low, line, kernel = tables(size)
    vmem = pl.BlockSpec(memory_space=pltpu.VMEM)
    return pl.pallas_call(
        functools.partial(exchange_body, size),
        out_shape=jax.ShapeDtypeStruct((rows, size), jnp.bfloat16),
        in_specs=[vmem] * STEPS + [pl.BlockSpec(memory_space=pl.ANY)] * 2 + [vmem] * 2,
        out_specs=vmem,
        scratch_shapes=[
            pltpu.VMEM((rows, LANES), jnp.float32),
            pltpu.VMEM((rows, 2 * LANES), jnp.bfloat16),
            pltpu.VMEM((rows, rows), jnp.bfloat16),
            pltpu.VMEM((rows, rows), jnp.bfloat16),
            pltpu.SemaphoreType.DMA((2,)),
        ],
        compiler_params=pltpu.CompilerParams(vmem_limit_bytes=58 * 2**20),
    )(*parts, high, low, line, kernel)


def factorize(margin):
    symmetric = 0.5 * (margin + margin.T)
    magnitude = jnp.abs(symmetric)
    gamma = jnp.mean(jnp.diagonal(magnitude)) + 1e-06
    regularized = jnp.diag(jnp.sum(magnitude, axis=1) + gamma) - symmetric
    factor = jnp.linalg.cholesky(regularized)
    identity = jnp.eye(symmetric.shape[0], dtype=jnp.float32)
    inverse = jax.scipy.linalg.solve_triangular(factor, identity, lower=True)
    return inverse.astype(jnp.bfloat16)


def to_slabs(flat, count, width):
    padded = jnp.pad(flat, ((0, 0), (0, count * width - flat.shape[1])))
    return lax.all_to_all(
        padded.reshape(count, width), AXES, split_axis=0, concat_axis=0, tiled=True
    )


def invert(symmetric, n):
    row = lax.broadcasted_iota(jnp.int32, (n, n), 0)
    column = lax.broadcasted_iota(jnp.int32, (n, n), 1)
    diagonal = row == column
    magnitude = jnp.abs(symmetric)
    gamma = jnp.sum(jnp.where(diagonal, magnitude, 0.0)) / n + 1e-06
    total = jnp.sum(magnitude, axis=1, keepdims=True) + gamma
    regularized = jnp.where(diagonal, total, 0.0) - symmetric
    value = jnp.concatenate([regularized, jnp.where(diagonal, 1.0, 0.0)], axis=1)
    below = lax.broadcasted_iota(jnp.int32, (n, 1), 0)
    for step in range(n - 1):
        here = slice(step, step + 1)
        scaled = value[here, :] / value[here, here]
        ratio = jnp.where(below > step, value[:, here], 0.0)
        value = value - ratio * scaled
    pivots = jnp.sum(jnp.where(diagonal, value[:, :n], 0.0), axis=1, keepdims=True)
    return (value[:, n:] * lax.rsqrt(pivots)).astype(jnp.bfloat16)


def flatten(wide, ref):
    wide[...] = ref[...].astype(jnp.float32)
    pieces = [wide[:, line, :] for line in range(wide.shape[1])]
    return jnp.concatenate(pieces, axis=1).astype(jnp.bfloat16)


def tail_body(count, groups, cells, orbital, exchange, back, orb_slab, exc_slab, wide, part, got,
              proj, send_sem, recv_sem):
    n = count
    me = lax.axis_index("orb") * groups + lax.axis_index("grp")

    def device(step):
        other = me + step
        other = jnp.where(other >= count, other - count, other)
        return other, (lax.div(other, groups), lax.rem(other, groups))

    def each(action):
        def body(step, carry):
            action(*device(step))
            return carry

        lax.fori_loop(1, count, body, 0)

    def send(source, target, slot, other, place):
        pltpu.make_async_remote_copy(
            src_ref=source,
            dst_ref=target.at[me],
            send_sem=send_sem.at[slot],
            recv_sem=recv_sem.at[slot],
            device_id=place,
            device_id_type=pl.DeviceIdType.MESH,
        ).start()

    def wait(target, slot):
        most = target.at[pl.ds(0, count - 1)]
        pltpu.make_async_copy(most, most, recv_sem.at[slot]).wait()
        pltpu.make_async_copy(most, most, send_sem.at[slot]).wait()

    barrier = pltpu.get_barrier_semaphore()
    each(
        lambda other, place: pl.semaphore_signal(
            barrier, inc=1, device_id=place, device_id_type=pl.DeviceIdType.MESH
        )
    )
    pl.semaphore_wait(barrier, count - 1)

    def slabs(other, place):
        send(orbital.at[other], orb_slab, 1, other, place)

    each(slabs)
    each(lambda other, place: send(exchange.at[other], exc_slab, 0, other, place))
    exc_slab[pl.ds(me, 1)] = exchange[pl.ds(me, 1)]
    orb_slab[pl.ds(me, 1)] = orbital[pl.ds(me, 1)]
    wait(orb_slab, 1)
    orb = flatten(wide, orb_slab)
    wait(exc_slab, 0)
    exc = flatten(wide, exc_slab)
    turned = (((1,), (1,)), ((), ()))
    both = lax.dot_general(orb, exc, turned, preferred_element_type=jnp.float32)
    both = both + lax.dot_general(exc, orb, turned, preferred_element_type=jnp.float32)
    both = both * (0.5 / cells)
    part[...] = jnp.concatenate([both[top : top + 8, :] for top in range(0, n, 8)], axis=1)
    each(lambda other, place: send(part, got, 2, other, place))
    got[pl.ds(me, 1)] = part[...][None]
    wait(got, 2)
    summed = jnp.sum(got[...], axis=0)
    symmetric = jnp.concatenate([summed[:, left : left + n] for left in range(0, n * n // 8, n)], axis=0)
    inverse = invert(symmetric, n)
    projected = dot(inverse, exc)
    for index in range(wide.shape[1]):
        wide[:, index, :] = projected[:, index * LANES : (index + 1) * LANES]
    proj[...] = wide[...].astype(jnp.bfloat16)
    each(lambda other, place: send(proj.at[other], back, 3, other, place))
    back[pl.ds(me, 1)] = proj[pl.ds(me, 1)]
    wait(back, 3)


def tail(orbital, exchange, cells):
    count, lines, _ = orbital.shape
    groups = lax.axis_size("grp")
    packed = count * count // 8
    vmem = pl.BlockSpec(memory_space=pltpu.VMEM)
    slab = pltpu.VMEM(orbital.shape, jnp.bfloat16)
    return pl.pallas_call(
        functools.partial(tail_body, count, groups, cells),
        out_shape=jax.ShapeDtypeStruct(orbital.shape, jnp.bfloat16),
        in_specs=[vmem] * 2,
        out_specs=vmem,
        scratch_shapes=[
            slab,
            slab,
            pltpu.VMEM(orbital.shape, jnp.float32),
            pltpu.VMEM((8, packed), jnp.float32),
            pltpu.VMEM((count, 8, packed), jnp.float32),
            slab,
            pltpu.SemaphoreType.DMA((4,)),
            pltpu.SemaphoreType.DMA((4,)),
        ],
        compiler_params=pltpu.CompilerParams(
            collective_id=0, has_side_effects=True, vmem_limit_bytes=56 * 2**20
        ),
    )(orbital, exchange)


def to_pieces(flat, count, lines):
    tall = flat.reshape(-1, LANES)
    padded = jnp.pad(tall, ((0, count * lines - tall.shape[0]), (0, 0)))
    return padded.reshape(count, lines, LANES)


def shards(orbitals):
    cells = orbitals.shape[1]
    size = round(cells ** (1.0 / 3.0))
    count = lax.axis_size("orb") * lax.axis_size("grp")
    tall = lax.optimization_barrier(orbitals.reshape(-1, LANES))
    parts = [tall] + [
        lax.optimization_barrier(shifted(tall, "orb", step)) for step in range(1, STEPS)
    ]
    parts = [part.reshape(size * size, size) for part in parts]
    compact = exchange_of(parts, size)
    if count <= LANES // 2 and count % 32 == 0:
        lines = -(-cells // (count * LANES * 16)) * 16
        back = tail(to_pieces(tall, count, lines), to_pieces(compact, count, lines), cells)
        return back.reshape(count * lines, LANES)[: cells // LANES].reshape(1, cells)
    width = -(-cells // (count * LANES)) * LANES
    orbital_slab = to_slabs(orbitals, count, width)
    exchange_slab = to_slabs(compact.reshape(1, cells), count, width)
    margin = lax.dot_general(
        orbital_slab, exchange_slab, (((1,), (1,)), ((), ())), preferred_element_type=jnp.float32
    )
    inverse = factorize(lax.psum(margin, AXES) / cells)
    projected = dot(inverse, exchange_slab).astype(jnp.bfloat16)
    back = lax.all_to_all(projected, AXES, split_axis=0, concat_axis=0, tiled=True)
    return back.reshape(1, count * width)[:, :cells]


def solution(mesh):
    spec = P(AXES, None)
    return jax.shard_map(shards, mesh=mesh, in_specs=(spec,), out_specs=spec, check_vma=False)
```

```python
import functools
import math

import jax
import jax.numpy as jnp
import ml_dtypes
import numpy as np
from jax import lax
from jax.experimental import pallas as pl
from jax.experimental.pallas import tpu as pltpu
from jax.sharding import PartitionSpec as P

STEPS = 3
LANES = 128
AXES = ("orb", "grp")


def shifted(value, axis, steps):
    count = lax.axis_size(axis)
    pairs = [(source, (source + steps) % count) for source in range(count)]
    return lax.ppermute(value, axis, pairs)


def halves(table):
    high = table.astype(ml_dtypes.bfloat16)
    low = (table - high.astype(np.float64)).astype(ml_dtypes.bfloat16)
    return high, low


@functools.lru_cache(maxsize=None)
def tables(size):
    index = np.arange(size)
    angle = 2.0 * math.pi / size * (index[:, None] * index[None, :] % size)
    table = np.cos(angle) + np.sin(angle)
    plane = halves(np.kron(table, table))
    line = np.zeros((LANES, LANES))
    block = np.kron(np.eye(STEPS), table)
    line[: block.shape[0], : block.shape[0]] = block
    line = np.concatenate(halves(line), axis=1)
    signed = np.where(index <= size // 2, index, index - size)
    square = (2.0 * math.pi / size * signed) ** 2
    total = square[:, None, None] + square[None, :, None] + square[None, None, :]
    safe = np.where(total > 0, total, 1.0)
    kernel = np.where(total > 0, 4.0 * (1.0 - np.exp(-0.25 * total)) / safe, 1.0) / size**3
    kernel = np.tile(kernel.reshape(size * size, size), (1, STEPS))
    spread = np.zeros((size * size, LANES), np.float32)
    spread[:, : kernel.shape[1]] = kernel
    return plane[0], plane[1], line, spread


def split(value):
    high = value.astype(jnp.bfloat16)
    return high, (value - high.astype(jnp.float32)).astype(jnp.bfloat16)


def dot(left, right):
    return jnp.dot(left, right, preferred_element_type=jnp.float32)


def line_transform(value, line):
    high, low = split(value)
    both = dot(high, line)
    return both[:, :LANES] + (both[:, LANES:] + dot(low, line[:, :LANES]))


def plane_transform(store, high_ref, low_ref, pair, rows, block, scale=None):
    for start in range(0, rows, block):
        here = pl.ds(start, block)
        both = dot(high_ref[here, :], pair[...])
        out = both[:, :LANES] + (both[:, LANES:] + dot(low_ref[here, :], pair[:, :LANES]))
        store[here, :] = out if scale is None else out * scale[here, :]


def put_pair(pair, value):
    high, low = split(value)
    pair[:, :LANES] = high
    pair[:, LANES:] = low


def exchange_body(size, *refs):
    parts = refs[:STEPS]
    high_far, low_far, line_ref, kernel_ref, out_ref, store, pair, high_ref, low_ref, sems = refs[STEPS:]
    copies = [
        pltpu.make_async_copy(high_far, high_ref, sems.at[0]),
        pltpu.make_async_copy(low_far, low_ref, sems.at[1]),
    ]
    for copy in copies:
        copy.start()
    rows = size * size
    block = rows // 5 if rows % 40 == 0 else rows
    values = [part[...].astype(jnp.float32) for part in parts]
    spare = jnp.zeros((rows, LANES - STEPS * size), jnp.float32)
    source = jnp.concatenate(values + [spare], axis=1)
    target = jnp.concatenate([values[0]] * STEPS + [spare], axis=1)
    line = line_ref[...]
    put_pair(pair, line_transform(target * source, line))
    for copy in copies:
        copy.wait()
    plane_transform(store, high_ref, low_ref, pair, rows, block, kernel_ref)
    put_pair(pair, store[...])
    plane_transform(store, high_ref, low_ref, pair, rows, block)
    term = source * line_transform(store[...], line)
    total = -term[:, :size]
    for step in range(1, STEPS):
        total = total - term[:, step * size : (step + 1) * size]
    out_ref[...] = total.astype(jnp.bfloat16)


def exchange_of(parts, size):
    rows = size * size
    high, low, line, kernel = tables(size)
    vmem = pl.BlockSpec(memory_space=pltpu.VMEM)
    return pl.pallas_call(
        functools.partial(exchange_body, size),
        out_shape=jax.ShapeDtypeStruct((rows, size), jnp.bfloat16),
        in_specs=[vmem] * STEPS + [pl.BlockSpec(memory_space=pl.ANY)] * 2 + [vmem] * 2,
        out_specs=vmem,
        scratch_shapes=[
            pltpu.VMEM((rows, LANES), jnp.float32),
            pltpu.VMEM((rows, 2 * LANES), jnp.bfloat16),
            pltpu.VMEM((rows, rows), jnp.bfloat16),
            pltpu.VMEM((rows, rows), jnp.bfloat16),
            pltpu.SemaphoreType.DMA((2,)),
        ],
        compiler_params=pltpu.CompilerParams(vmem_limit_bytes=58 * 2**20),
    )(*parts, high, low, line, kernel)


def factorize(margin):
    symmetric = 0.5 * (margin + margin.T)
    magnitude = jnp.abs(symmetric)
    gamma = jnp.mean(jnp.diagonal(magnitude)) + 1e-06
    regularized = jnp.diag(jnp.sum(magnitude, axis=1) + gamma) - symmetric
    factor = jnp.linalg.cholesky(regularized)
    identity = jnp.eye(symmetric.shape[0], dtype=jnp.float32)
    inverse = jax.scipy.linalg.solve_triangular(factor, identity, lower=True)
    return inverse.astype(jnp.bfloat16)


def to_slabs(flat, count, width):
    padded = jnp.pad(flat, ((0, 0), (0, count * width - flat.shape[1])))
    return lax.all_to_all(
        padded.reshape(count, width), AXES, split_axis=0, concat_axis=0, tiled=True
    )


def invert(symmetric, n):
    row = lax.broadcasted_iota(jnp.int32, (n, n), 0)
    column = lax.broadcasted_iota(jnp.int32, (n, n), 1)
    diagonal = row == column
    magnitude = jnp.abs(symmetric)
    gamma = jnp.sum(jnp.where(diagonal, magnitude, 0.0)) / n + 1e-06
    total = jnp.sum(magnitude, axis=1, keepdims=True) + gamma
    regularized = jnp.where(diagonal, total, 0.0) - symmetric
    value = jnp.concatenate([regularized, jnp.where(diagonal, 1.0, 0.0)], axis=1)
    below = lax.broadcasted_iota(jnp.int32, (n, 1), 0)
    for step in range(n - 1):
        here = slice(step, step + 1)
        scaled = value[here, :] / value[here, here]
        ratio = jnp.where(below > step, value[:, here], 0.0)
        value = value - ratio * scaled
    pivots = jnp.sum(jnp.where(diagonal, value[:, :n], 0.0), axis=1, keepdims=True)
    return (value[:, n:] * lax.rsqrt(pivots)).astype(jnp.bfloat16)


def flatten(wide, ref):
    wide[...] = ref[...].astype(jnp.float32)
    pieces = [wide[:, line, :] for line in range(wide.shape[1])]
    return jnp.concatenate(pieces, axis=1).astype(jnp.bfloat16)


def tail_body(count, groups, cells, orbital, exchange, back, orb_slab, exc_slab, wide, part, got,
              proj, send_sem, recv_sem):
    n = count
    me = lax.axis_index("orb") * groups + lax.axis_index("grp")

    def device(step):
        other = me + step
        other = jnp.where(other >= count, other - count, other)
        return other, (lax.div(other, groups), lax.rem(other, groups))

    def each(action):
        def body(step, carry):
            action(*device(step))
            return carry

        lax.fori_loop(1, count, body, 0, unroll=True)

    def send(source, target, slot, other, place):
        pltpu.make_async_remote_copy(
            src_ref=source,
            dst_ref=target.at[me],
            send_sem=send_sem.at[slot],
            recv_sem=recv_sem.at[slot],
            device_id=place,
            device_id_type=pl.DeviceIdType.MESH,
        ).start()

    def wait(target, slot):
        most = target.at[pl.ds(0, count - 1)]
        pltpu.make_async_copy(most, most, recv_sem.at[slot]).wait()
        pltpu.make_async_copy(most, most, send_sem.at[slot]).wait()

    barrier = pltpu.get_barrier_semaphore()
    each(
        lambda other, place: pl.semaphore_signal(
            barrier, inc=1, device_id=place, device_id_type=pl.DeviceIdType.MESH
        )
    )
    pl.semaphore_wait(barrier, count - 1)

    def slabs(other, place):
        send(orbital.at[other], orb_slab, 1, other, place)

    each(slabs)
    each(lambda other, place: send(exchange.at[other], exc_slab, 0, other, place))
    exc_slab[pl.ds(me, 1)] = exchange[pl.ds(me, 1)]
    orb_slab[pl.ds(me, 1)] = orbital[pl.ds(me, 1)]
    wait(orb_slab, 1)
    orb = flatten(wide, orb_slab)
    wait(exc_slab, 0)
    exc = flatten(wide, exc_slab)
    turned = (((1,), (1,)), ((), ()))
    both = lax.dot_general(orb, exc, turned, preferred_element_type=jnp.float32)
    both = both + lax.dot_general(exc, orb, turned, preferred_element_type=jnp.float32)
    both = both * (0.5 / cells)
    part[...] = jnp.concatenate([both[top : top + 8, :] for top in range(0, n, 8)], axis=1)
    each(lambda other, place: send(part, got, 2, other, place))
    got[pl.ds(me, 1)] = part[...][None]
    wait(got, 2)
    summed = jnp.sum(got[...], axis=0)
    symmetric = jnp.concatenate([summed[:, left : left + n] for left in range(0, n * n // 8, n)], axis=0)
    inverse = invert(symmetric, n)
    projected = dot(inverse, exc)
    for index in range(wide.shape[1]):
        wide[:, index, :] = projected[:, index * LANES : (index + 1) * LANES]
    proj[...] = wide[...].astype(jnp.bfloat16)
    each(lambda other, place: send(proj.at[other], back, 3, other, place))
    back[pl.ds(me, 1)] = proj[pl.ds(me, 1)]
    wait(back, 3)


def tail(orbital, exchange, cells):
    count, lines, _ = orbital.shape
    groups = lax.axis_size("grp")
    packed = count * count // 8
    vmem = pl.BlockSpec(memory_space=pltpu.VMEM)
    slab = pltpu.VMEM(orbital.shape, jnp.bfloat16)
    return pl.pallas_call(
        functools.partial(tail_body, count, groups, cells),
        out_shape=jax.ShapeDtypeStruct(orbital.shape, jnp.bfloat16),
        in_specs=[vmem] * 2,
        out_specs=vmem,
        scratch_shapes=[
            slab,
            slab,
            pltpu.VMEM(orbital.shape, jnp.float32),
            pltpu.VMEM((8, packed), jnp.float32),
            pltpu.VMEM((count, 8, packed), jnp.float32),
            slab,
            pltpu.SemaphoreType.DMA((4,)),
            pltpu.SemaphoreType.DMA((4,)),
        ],
        compiler_params=pltpu.CompilerParams(
            collective_id=0, has_side_effects=True, vmem_limit_bytes=56 * 2**20
        ),
    )(orbital, exchange)


def to_pieces(flat, count, lines):
    tall = flat.reshape(-1, LANES)
    padded = jnp.pad(tall, ((0, count * lines - tall.shape[0]), (0, 0)))
    return padded.reshape(count, lines, LANES)


def shards(orbitals):
    cells = orbitals.shape[1]
    size = round(cells ** (1.0 / 3.0))
    count = lax.axis_size("orb") * lax.axis_size("grp")
    tall = lax.optimization_barrier(orbitals.reshape(-1, LANES))
    parts = [tall] + [
        lax.optimization_barrier(shifted(tall, "orb", step)) for step in range(1, STEPS)
    ]
    parts = [part.reshape(size * size, size) for part in parts]
    compact = exchange_of(parts, size)
    if count <= LANES // 2 and count % 32 == 0:
        lines = -(-cells // (count * LANES * 16)) * 16
        back = tail(to_pieces(tall, count, lines), to_pieces(compact, count, lines), cells)
        return back.reshape(count * lines, LANES)[: cells // LANES].reshape(1, cells)
    width = -(-cells // (count * LANES)) * LANES
    orbital_slab = to_slabs(orbitals, count, width)
    exchange_slab = to_slabs(compact.reshape(1, cells), count, width)
    margin = lax.dot_general(
        orbital_slab, exchange_slab, (((1,), (1,)), ((), ())), preferred_element_type=jnp.float32
    )
    inverse = factorize(lax.psum(margin, AXES) / cells)
    projected = dot(inverse, exchange_slab).astype(jnp.bfloat16)
    back = lax.all_to_all(projected, AXES, split_axis=0, concat_axis=0, tiled=True)
    return back.reshape(1, count * width)[:, :cells]


def solution(mesh):
    spec = P(AXES, None)
    return jax.shard_map(shards, mesh=mesh, in_specs=(spec,), out_specs=spec, check_vma=False)
```
